128 devices in a mesh: dp: 8 (over y, x_hi), tensor: 16 (over z, x_lo, core).
Axes of the slice: x: 4 (x_hi: 2, x_lo: 2; x = x_hi * 2 + x_lo), y: 4, z: 4, core: 2. Of those that a mesh axis runs over, the one named last changes fastest.
Arguments:
- acts: bfloat16 [64, 512, 28672], P('dp', None, 'tensor'), may hold values from -6 to 6
- grads: bfloat16 [64, 512, 8192], P('dp', None, 'tensor'), may hold values from -6 to 6
- proj_in: bfloat16 [28672, 64], P('tensor'), may hold values from -0.03125 to 0.03125
- proj_out: bfloat16 [8192, 64], P('tensor'), may hold values from -0.0625 to 0.0625
- queries: float32 [512, 4096], P('dp', 'tensor'), may hold values from -6 to 6
Outputs:
- scores: float32 [64, 512], P('dp')
The draws below stay inside these ranges and needn't reach their ends.
All inputs are finite; a program needn't handle non-finite values.
Results may differ from the reference program's by a relative error of at most 0.0003.
Values sent between devices are 32-bit elements; how exact they have to be, the bound alone decides.
No kernel may reach another device: no remote copies, remote signals or barrier semaphores. Data moves between devices by JAX's collectives and lax.ppermute only.
A program may use at most 128 MiB of HBM per device.

```python
import jax
import jax.numpy as jnp
from jax import lax

D = 8192
FF = 28672
RANK = 64
LENGTH = 512
EXAMPLES = 64
QUERIES = 512


def level_of(rng, shape, shards, smallest, high):
    level = 1.0
    for position, blocks in shards:
        steps = jax.random.uniform(jax.random.fold_in(jax.random.fold_in(rng, 6), position), (blocks,), jnp.float32, smallest / len(shards), high / len(shards))
        level = level * jnp.repeat(jnp.exp(steps), shape[position] // blocks).reshape((-1,) + (1,) * (len(shape) - 1 - position))
    return level


def noise(rng, shape, deviation, limit, pieces=(), kind=jnp.bfloat16):
    result = deviation * jax.random.normal(rng, shape, jnp.float32)
    if pieces:
        result = result * level_of(rng, shape, pieces, -0.22, 0.18)
    return jnp.clip(result, -limit, limit).astype(kind)


def setup_inputs(seed: int = 0) -> dict:
    keys = jax.random.split(jax.random.key(seed), 6)
    acts = noise(keys[0], (EXAMPLES, LENGTH, FF), 1.0, 6.0, ((0, 8), (2, 16)))
    grads = noise(keys[1], (EXAMPLES, LENGTH, D), 1.0, 6.0, ((0, 8), (2, 16)))
    proj_in = noise(keys[2], (FF, RANK), FF ** -0.5, 0.03125, ((0, 16),))
    proj_out = noise(keys[3], (D, RANK), D ** -0.5, 0.0625, ((0, 16),))
    queries = noise(keys[4], (QUERIES, RANK * RANK), 1.0, 6.0, ((0, 8), (1, 16)), jnp.float32)
    return dict(acts=acts, grads=grads, proj_in=proj_in, proj_out=proj_out, queries=queries)


def reference(acts, grads, proj_in, proj_out, queries):
    side_in = jnp.dot(acts.reshape(EXAMPLES * LENGTH, FF), proj_in, preferred_element_type=jnp.float32)
    side_out = jnp.dot(grads.reshape(EXAMPLES * LENGTH, D), proj_out, preferred_element_type=jnp.float32)
    side_in = side_in.reshape(EXAMPLES, LENGTH, RANK)
    side_out = side_out.reshape(EXAMPLES, LENGTH, RANK)
    encoding = jnp.einsum("eti,etj->eij", side_out, side_in, precision=lax.Precision.HIGHEST)
    encoding = (encoding * (LENGTH ** -0.5)).reshape(EXAMPLES, RANK * RANK)
    scores = jnp.einsum("ek,qk->eq", encoding, queries, precision=lax.Precision.HIGHEST)
    return scores / RANK
```

```python
import functools

import jax
import jax.numpy as jnp
from jax import lax
from jax.experimental import pallas as pl
from jax.experimental.pallas import tpu as pltpu
from jax.sharding import PartitionSpec as P

ROWS = 128
NT = (((1,), (1,)), ((), ()))
TN = (((0,), (0,)), ((), ()))


def place():
    t = lax.axis_index("tensor")
    return t // 4, (t // 2) % 2, t % 2


def example_of(position, x_first, z, x):
    if x_first:
        dx, dz = position // 4, position % 4
    else:
        dz, dx = position // 2, position % 2
    return 2 * ((z + dz) % 4) + (x + dx) % 2


def project_kernel(half, mine, x_first, cuts, acts, grads, pin, pout, *rest):
    received = rest[0] if mine else None
    outs = rest[1:-3] if mine else rest[:-3]
    held_a, held_g, sem = rest[-3:]
    z, x, core = place()
    part = core if mine else 1 - core
    row = half * 2 * ROWS + part * ROWS
    copies = []
    for p in range(8):
        e = example_of(p, x_first, z, x)
        where = pl.ds(pl.multiple_of(row, ROWS), ROWS)
        ca = pltpu.make_async_copy(acts.at[e, where, :], held_a.at[pl.ds(p * ROWS, ROWS), :], sem.at[0, p])
        cg = pltpu.make_async_copy(grads.at[e, where, :], held_g.at[pl.ds(p * ROWS, ROWS), :], sem.at[1, p])
        cg.start()
        ca.start()
        copies.append((ca, cg))
    for g in range(2):
        for ca, cg in copies[4 * g : 4 * g + 4]:
            cg.wait()
            ca.wait()
        rows = pl.ds(g * 4 * ROWS, 4 * ROWS)
        so = lax.dot_general(held_g[rows, :], pout[...], NT, preferred_element_type=jnp.float32)
        si = lax.dot_general(held_a[rows, :], pin[...], NT, preferred_element_type=jnp.float32)
        both = jnp.concatenate([so, si], axis=1).reshape(4, ROWS, 128)
        if mine:
            both = both + received[pl.ds(4 * g, 4)]
        for k, ref in enumerate(outs):
            lo, hi = max(cuts[k], 4 * g), min(cuts[k + 1], 4 * g + 4)
            if lo < hi:
                ref[lo - cuts[k] : hi - cuts[k]] = both[lo - 4 * g : hi - 4 * g]


def project(half, mine, x_first, cuts, acts, grads, pin, pout, received=None):
    any_space = pl.BlockSpec(memory_space=pl.ANY)
    vmem = pl.BlockSpec(memory_space=pltpu.VMEM)
    args = (acts, grads, pin, pout) + ((received,) if mine else ())
    return pl.pallas_call(
        functools.partial(project_kernel, half, mine, x_first, cuts),
        out_shape=[
            jax.ShapeDtypeStruct((b - a, ROWS, 128), jnp.float32) for a, b in zip(cuts, cuts[1:])
        ],
        in_specs=[any_space, any_space, vmem, vmem] + ([vmem] if mine else []),
        out_specs=[vmem] * (len(cuts) - 1),
        scratch_shapes=[
            pltpu.VMEM((8 * ROWS, acts.shape[2]), acts.dtype),
            pltpu.VMEM((8 * ROWS, grads.shape[2]), grads.dtype),
            pltpu.SemaphoreType.DMA((2, 8)),
        ],
        compiler_params=pltpu.CompilerParams(vmem_limit_bytes=40 << 20),
        name=f"project_{half}_{'keep' if mine else 'send'}",
    )(*args)


def encode_kernel(own0, a1, a2, a3, own1, b1, out, enc):
    z, x, _ = place()
    m0 = (own0[...] + a2[...]) + (a1[...] + a3[...])
    m1 = own1[...] + b1[...]
    m = jnp.concatenate([m0, m1], axis=0)
    enc[...] = lax.dot_general(
        m[:, :64], m[:, 64:], TN, precision=lax.Precision.HIGHEST, preferred_element_type=jnp.float32
    )
    for p in range(8):
        g = example_of(p, True, z, x)
        out[p] = enc[pl.ds(pl.multiple_of(8 * g, 8), 8), :]


def encode(*args):
    return pl.pallas_call(
        encode_kernel,
        out_shape=jax.ShapeDtypeStruct((8, 8, 64), jnp.float32),
        scratch_shapes=[pltpu.VMEM((64, 64), jnp.float32)],
        name="encode",
    )(*args)


def score_kernel(scale, own, other, r1, r2, r3, q_own, q_other, out, tiles):
    z, x, core = place()
    y = lax.axis_index("dp") // 2
    for dz, pair in enumerate((None, r1, r2, r3)):
        for dx in range(2):
            e = 2 * ((z - dz + 4) % 4) + (x + dx) % 2
            tile = (own, other)[dx][0] if pair is None else pair[dx]
            tiles[pl.ds(pl.multiple_of(8 * e, 8), 8), :] = tile
    low = jnp.concatenate([tiles[pl.ds(i, 8, stride=8), :] for i in range(4)], axis=1)
    high = jnp.concatenate([tiles[pl.ds(i, 8, stride=8), :] for i in range(4, 8)], axis=1)
    mine = jnp.where(core == 0, low, high) * scale
    theirs = jnp.where(core == 0, high, low) * scale
    for dy in range(4):
        rows = pl.ds(128 * dy, 128)
        a = lax.dot_general(
            mine, q_own[rows, :], NT, precision=lax.Precision.HIGHEST, preferred_element_type=jnp.float32
        )
        b = lax.dot_general(
            theirs, q_other[rows, :], NT, precision=lax.Precision.HIGHEST, preferred_element_type=jnp.float32
        )
        out[:, pl.ds(pl.multiple_of(128 * ((y - dy + 4) % 4), 128), 128)] = a + b


def score(scale, *args):
    return pl.pallas_call(
        functools.partial(score_kernel, scale),
        out_shape=jax.ShapeDtypeStruct((8, 512), jnp.float32),
        scratch_shapes=[pltpu.VMEM((64, 64), jnp.float32)],
        name="score",
    )(*args)


def move(value, axis, to):
    n = lax.axis_size(axis)
    return lax.ppermute(value, axis, [(i, to(i)) for i in range(n)])


def to_core(value):
    return move(value, "tensor", lambda t: t ^ 1)


def to_x(value):
    return move(value, "tensor", lambda t: t ^ 2)


def to_z(value, dz):
    return move(value, "tensor", lambda t: (t + 4 * dz) % 16)


def per_device(acts, grads, proj_in, proj_out, queries):
    length = acts.shape[1]
    rank = proj_in.shape[1]
    pin, pout = proj_in.T, proj_out.T

    with jax.named_scope("sides"):
        (send0,) = project(0, False, True, (0, 8), acts, grads, pin, pout)
        got0 = to_core(send0)
        (send1,) = project(1, False, False, (0, 8), acts, grads, pin, pout)
        got1 = to_core(send1)
        near0, far0 = project(0, True, True, (0, 4, 8), acts, grads, pin, pout, got0)
        other0 = to_x(far0)
        near1, z1, z2, z3 = project(1, True, False, (0, 2, 4, 6, 8), acts, grads, pin, pout, got1)
        z1, z2, z3 = to_z(z1, 1), to_z(z2, 2), to_z(z3, 3)
        sum0 = near0 + other0
        w1, w2, w3 = to_z(sum0[1], 1), to_z(sum0[2], 2), to_z(sum0[3], 3)
        sum1 = (near1 + z2) + (z1 + z3)
        v1 = to_x(sum1[1])

    with jax.named_scope("queries"):
        x_hi = lax.axis_index("dp") % 2
        beside = move(queries, "dp", lambda d: d ^ 1)
        pair = jnp.where(
            x_hi == 0, jnp.concatenate([queries, beside]), jnp.concatenate([beside, queries])
        )
        rest = [move(pair, "dp", lambda d, dy=dy: (d + 2 * dy) % 8) for dy in (1, 2, 3)]
        q_own = jnp.concatenate([pair] + rest)
        q_other = to_core(q_own)

    with jax.named_scope("encode"):
        encoded = encode(sum0[0], w1, w2, w3, sum1[0], v1)
        encoded = encoded + to_core(encoded)
        keep, send = encoded[:4], encoded[4:]
        other = to_x(send)
        out = [to_z(jnp.stack([keep[dz], other[dz]]), dz) for dz in (1, 2, 3)]

    with jax.named_scope("scores"):
        part = score(length ** (-0.5) / rank, keep, other, *out, q_own, q_other)
        part = part + to_x(part)
        s1, s2, s3 = to_z(part, 1), to_z(part, 2), to_z(part, 3)
        return (part + s2) + (s1 + s3)


def solution(mesh):
    in_specs = (
        P("dp", None, "tensor"),
        P("dp", None, "tensor"),
        P("tensor", None),
        P("tensor", None),
        P("dp", "tensor"),
    )
    out_specs = P("dp", None)
    return jax.shard_map(
        per_device, mesh=mesh, in_specs=in_specs, out_specs=out_specs, check_vma=False
    )
```

```python
import functools

import jax
import jax.numpy as jnp
from jax import lax
from jax.experimental import pallas as pl
from jax.experimental.pallas import tpu as pltpu
from jax.sharding import PartitionSpec as P

NT = (((1,), (1,)), ((), ()))
CHIPS = [[c + 2 * chip for chip in range(8)] for c in range(2)]


def project_kernel(mine, acts, grads, pin, pout, *rest):
    if mine:
        out, held_a, held_g, held_pin, held_pout, sem, p_sem = rest
    else:
        passed, out, passed_out, held_a, held_g, held_pin, held_pout, sem, p_sem = rest
    examples, rank, rows = out.shape[0], out.shape[1] // 2, out.shape[2]
    core = lax.axis_index("tensor") % 2
    part = core if mine else 1 - core
    copies = [
        pltpu.make_async_copy(pout, held_pout, p_sem.at[0]),
        pltpu.make_async_copy(pin, held_pin, p_sem.at[1]),
    ]
    for e in range(examples):
        for k in range(2):
            here = pl.ds(pl.multiple_of(part * rows + k * (rows // 2), rows // 2), rows // 2)
            to = pl.ds(e * rows + k * (rows // 2), rows // 2)
            copies.append(pltpu.make_async_copy(grads.at[e, here, :], held_g.at[to, :], sem.at[0, e, k]))
            copies.append(pltpu.make_async_copy(acts.at[e, here, :], held_a.at[to, :], sem.at[1, e, k]))
    for copy in copies:
        copy.start()
    if not mine:
        passed_out[...] = passed[...]
    for copy in copies[:2]:
        copy.wait()
    for e in range(0, examples, 2):
        for copy in copies[2 + 4 * e : 10 + 4 * e]:
            copy.wait()
        block = pl.ds(e * rows, 2 * rows)
        so = lax.dot_general(held_pout[...], held_g[block, :], NT, preferred_element_type=jnp.float32)
        si = lax.dot_general(held_pin[...], held_a[block, :], NT, preferred_element_type=jnp.float32)
        for k in range(2):
            out[e + k, :rank, :] = so[:, k * rows : (k + 1) * rows]
            out[e + k, rank:, :] = si[:, k * rows : (k + 1) * rows]


def project(mine, acts, grads, pin, pout, *passed):
    examples, length, width_in = acts.shape
    rows = length // 2
    hbm = pl.BlockSpec(memory_space=pl.ANY)
    vmem = pl.BlockSpec(memory_space=pltpu.VMEM)
    return pl.pallas_call(
        functools.partial(project_kernel, mine),
        out_shape=[
            jax.ShapeDtypeStruct((examples, 2 * pin.shape[0], rows), jnp.float32),
            *(jax.ShapeDtypeStruct(p.shape, p.dtype) for p in passed),
        ],
        in_specs=[hbm] * 4 + [vmem] * len(passed),
        out_specs=[vmem] * (1 + len(passed)),
        scratch_shapes=[
            pltpu.VMEM((examples * rows, width_in), acts.dtype),
            pltpu.VMEM((examples * rows, grads.shape[2]), grads.dtype),
            pltpu.VMEM(pin.shape, pin.dtype),
            pltpu.VMEM(pout.shape, pout.dtype),
            pltpu.SemaphoreType.DMA((2, examples, 2)),
            pltpu.SemaphoreType.DMA((2,)),
        ],
        compiler_params=pltpu.CompilerParams(vmem_limit_bytes=51 << 20),
        name="project_own" if mine else "project_other",
    )(acts, grads, pin, pout, *passed)


def merge_kernel(own, got, queries, beside, total, pair):
    total[...] = own[...] + got[...]
    n = queries.shape[0]
    x_hi = lax.axis_index("dp") % 2
    pair[pl.ds(pl.multiple_of(x_hi * n, n), n), :] = queries[...]
    pair[pl.ds(pl.multiple_of((1 - x_hi) * n, n), n), :] = beside[...]


def merge(own, got, queries, beside):
    n, k = queries.shape
    vmem = pl.BlockSpec(memory_space=pltpu.VMEM)
    return pl.pallas_call(
        merge_kernel,
        out_shape=[
            jax.ShapeDtypeStruct(own.shape, jnp.float32),
            jax.ShapeDtypeStruct((2 * n, k), jnp.float32),
        ],
        in_specs=[vmem] * 4,
        out_specs=[vmem] * 2,
        compiler_params=pltpu.CompilerParams(vmem_limit_bytes=16 << 20),
        name="merge",
    )(own, got, queries, beside)


def encode_kernel(sides, out):
    total = ((sides[0] + sides[1]) + (sides[2] + sides[3])) + ((sides[4] + sides[5]) + (sides[6] + sides[7]))
    rank = total.shape[0] // 2
    enc = lax.dot_general(
        total[:rank], total[rank:], NT, precision=lax.Precision.HIGHEST, preferred_element_type=jnp.float32
    )
    take = rank // out.shape[0]
    out[...] = jnp.zeros_like(out)
    for t in range(out.shape[0]):
        out[t, :take, :rank] = enc[take * t : take * (t + 1), :]


def encode(sides):
    return pl.pallas_call(
        encode_kernel,
        out_shape=jax.ShapeDtypeStruct((16, 8, 128), jnp.float32),
        in_specs=[pl.BlockSpec(memory_space=pltpu.VMEM)],
        out_specs=pl.BlockSpec(memory_space=pltpu.VMEM),
        compiler_params=pltpu.CompilerParams(vmem_limit_bytes=8 << 20),
        name="encode",
    )(sides)


def score_kernel(scale, slices, q0, q1, q2, q3, out, tiles):
    y = lax.axis_index("dp") // 2
    for e in range(8):
        tiles[pl.ds(8 * e, 8), :] = slices[2 * e] + slices[2 * e + 1]
    enc = jnp.concatenate([tiles[pl.ds(i, 8, stride=8), :][:, :64] for i in range(4)], axis=1) * scale
    for dy, queries in enumerate((q0, q1, q2, q3)):
        part = lax.dot_general(
            enc, queries[...], NT, precision=lax.Precision.HIGHEST, preferred_element_type=jnp.float32
        )
        columns = pl.ds(pl.multiple_of((y - dy + 4) % 4 * 128, 128), 128)
        for t in range(out.shape[0]):
            out[t, :, columns] = part


def score(scale, slices, *queries):
    return pl.pallas_call(
        functools.partial(score_kernel, scale),
        out_shape=jax.ShapeDtypeStruct((16, 8, 4 * queries[0].shape[0]), jnp.float32),
        in_specs=[pl.BlockSpec(memory_space=pltpu.VMEM)] * 5,
        out_specs=pl.BlockSpec(memory_space=pltpu.VMEM),
        scratch_shapes=[pltpu.VMEM((64, 128), jnp.float32)],
        compiler_params=pltpu.CompilerParams(vmem_limit_bytes=8 << 20),
        name="score",
    )(slices, *queries)


def per_device(acts, grads, proj_in, proj_out, queries):
    length = acts.shape[1]
    rank = proj_in.shape[1]
    pin, pout = proj_in.T, proj_out.T

    with jax.named_scope("sides"):
        other, queries = project(False, acts, grads, pin, pout, queries)
        beside = lax.ppermute(queries, "dp", [(d, d ^ 1) for d in range(8)])
        got = lax.ppermute(other, "tensor", [(t, t ^ 1) for t in range(16)])
        (own,) = project(True, acts, grads, pin, pout)
        total, pair = merge(own, got, queries, beside)
        sides = lax.all_to_all(total, "tensor", 0, 0, tiled=True, axis_index_groups=CHIPS)

    with jax.named_scope("queries"):
        wide = [pair] + [
            lax.ppermute(pair, "dp", [(d, (d + 2 * dy) % 8) for d in range(8)]) for dy in (1, 2, 3)
        ]

    with jax.named_scope("encode"):
        slices = lax.all_to_all(encode(sides), "tensor", 0, 0, tiled=True)

    with jax.named_scope("scores"):
        parts = lax.all_to_all(
            score(length ** (-0.5) / rank, slices, *wide), "tensor", 0, 0, tiled=True
        )
        return jnp.sum(parts, axis=0)


def solution(mesh):
    in_specs = (
        P("dp", None, "tensor"),
        P("dp", None, "tensor"),
        P("tensor", None),
        P("tensor", None),
        P("dp", "tensor"),
    )
    out_specs = P("dp", None)
    return jax.shard_map(
        per_device, mesh=mesh, in_specs=in_specs, out_specs=out_specs, check_vma=False
    )
```

```python
import functools

import jax
import jax.numpy as jnp
from jax import lax
from jax.experimental import pallas as pl
from jax.experimental.pallas import tpu as pltpu
from jax.sharding import PartitionSpec as P

NT = (((1,), (1,)), ((), ()))
CHIPS = [[c + 2 * chip for chip in range(8)] for c in range(2)]
HBM = pl.BlockSpec(memory_space=pltpu.HBM)
VMEM = pl.BlockSpec(memory_space=pltpu.VMEM)


def in_hbm(value):
    return pltpu.with_memory_space_constraint(value, pltpu.HBM)


def limit(mib):
    return pltpu.CompilerParams(vmem_limit_bytes=mib << 20)


def shape(*dims):
    return jax.ShapeDtypeStruct(dims, jnp.float32)


def project_kernel(mine, acts, grads, pin, pout, *rest):
    if mine:
        out, held_a, held_g, held_pin, held_pout, sem, p_sem = rest
    else:
        queries, out, passed, held_a, held_g, held_pin, held_pout, sem, p_sem = rest
    examples, rank, rows = out.shape[0], out.shape[1] // 2, out.shape[2]
    core = lax.axis_index("tensor") % 2
    part = core if mine else 1 - core
    weights = [
        pltpu.make_async_copy(pout, held_pout, p_sem.at[0]),
        pltpu.make_async_copy(pin, held_pin, p_sem.at[1]),
    ]
    blocks = []
    for e in range(examples):
        for k in range(2):
            here = pl.ds(pl.multiple_of(part * rows + k * (rows // 2), rows // 2), rows // 2)
            to = pl.ds(e * rows + k * (rows // 2), rows // 2)
            blocks.append(pltpu.make_async_copy(grads.at[e, here, :], held_g.at[to, :], sem.at[0, e, k]))
            blocks.append(pltpu.make_async_copy(acts.at[e, here, :], held_a.at[to, :], sem.at[1, e, k]))
    for copy in weights + blocks[:8]:
        copy.start()
    for copy in weights:
        copy.wait()
    if not mine:
        across = pltpu.make_async_copy(queries, passed, p_sem.at[2])
        blocks.append(across)
    for copy in blocks[8:]:
        copy.start()
    for e in range(0, examples, 2):
        for copy in blocks[4 * e : 8 + 4 * e]:
            copy.wait()
        block = pl.ds(e * rows, 2 * rows)
        so = lax.dot_general(held_pout[...], held_g[block, :], NT, preferred_element_type=jnp.float32)
        si = lax.dot_general(held_pin[...], held_a[block, :], NT, preferred_element_type=jnp.float32)
        for k in range(2):
            out[e + k, :rank, :] = so[:, k * rows : (k + 1) * rows]
            out[e + k, rank:, :] = si[:, k * rows : (k + 1) * rows]
    if not mine:
        across.wait()


def project(mine, acts, grads, pin, pout, *passed):
    examples, length, width_in = acts.shape
    rows = length // 2
    return pl.pallas_call(
        functools.partial(project_kernel, mine),
        out_shape=[shape(examples, 2 * pin.shape[0], rows)] + [shape(*p.shape) for p in passed],
        in_specs=[HBM] * (4 + len(passed)),
        out_specs=[VMEM] * (1 + len(passed)),
        scratch_shapes=[
            pltpu.VMEM((examples * rows, width_in), acts.dtype),
            pltpu.VMEM((examples * rows, grads.shape[2]), grads.dtype),
            pltpu.VMEM(pin.shape, pin.dtype),
            pltpu.VMEM(pout.shape, pout.dtype),
            pltpu.SemaphoreType.DMA((2, examples, 2)),
            pltpu.SemaphoreType.DMA((3,)),
        ],
        compiler_params=limit(24),
        name="project_own" if mine else "project_other",
    )(*(in_hbm(v) for v in (acts, grads, pin, pout) + passed))


def merge_kernel(own, got, queries, beside, total, pair):
    total[...] = own[...] + got[...]
    n = queries.shape[0]
    x_hi = lax.axis_index("dp") % 2
    pair[pl.ds(pl.multiple_of(x_hi * n, n), n), :] = queries[...]
    pair[pl.ds(pl.multiple_of((1 - x_hi) * n, n), n), :] = beside[...]


def merge(own, got, queries, beside):
    n, k = queries.shape
    return pl.pallas_call(
        merge_kernel,
        out_shape=[shape(*own.shape), shape(2 * n, k)],
        in_specs=[VMEM] * 4,
        out_specs=[VMEM] * 2,
        compiler_params=limit(8),
        name="merge",
    )(own, got, queries, beside)


def encode_kernel(sides, q0, q1, q2, q3, out, near):
    for dy, block in enumerate((q0, q1, q2, q3)):
        near[pl.ds(dy * block.shape[0], block.shape[0]), :] = block[...]
    total = ((sides[0] + sides[1]) + (sides[2] + sides[3])) + ((sides[4] + sides[5]) + (sides[6] + sides[7]))
    rank = total.shape[0] // 2
    enc = lax.dot_general(
        total[:rank], total[rank:], NT, precision=lax.Precision.HIGHEST, preferred_element_type=jnp.float32
    )
    out[...] = jnp.zeros_like(out)
    for t in range(16):
        out[t, :, :rank] = enc[8 * (t // 2) : 8 * (t // 2) + 8, :]


def encode(sides, *blocks):
    n, k = blocks[0].shape
    return pl.pallas_call(
        encode_kernel,
        out_shape=[shape(16, 8, 128), shape(4 * n, k)],
        in_specs=[VMEM] * 5,
        out_specs=[VMEM] * 2,
        compiler_params=limit(8),
        name="encode",
    )(sides, *blocks)


def score_kernel(scale, slices, near, far, out, tiles):
    core = lax.axis_index("tensor") % 2
    y = lax.axis_index("dp") // 2
    for e in range(8):
        tiles[pl.ds(8 * e, 8), :] = slices[2 * e] + slices[2 * e + 1]
    rows = [tiles[pl.ds(i, 8, stride=8), :][:, :64] for i in range(8)]
    low, high = jnp.concatenate(rows[:4], axis=1), jnp.concatenate(rows[4:], axis=1)
    mine = jnp.where(core == 0, low, high) * scale
    theirs = jnp.where(core == 0, high, low) * scale

    def dot(enc, block):
        return lax.dot_general(
            enc, block[...], NT, precision=lax.Precision.HIGHEST, preferred_element_type=jnp.float32
        )

    part = dot(mine, near) + dot(theirs, far)
    for dy in range(4):
        columns = pl.ds(pl.multiple_of((y - dy + 4) % 4 * 128, 128), 128)
        for g in range(8):
            out[g, :, columns] = part[:, 128 * dy : 128 * dy + 128]


def score(scale, slices, near, far):
    return pl.pallas_call(
        functools.partial(score_kernel, scale),
        out_shape=shape(8, 8, 512),
        in_specs=[VMEM] * 3,
        out_specs=VMEM,
        scratch_shapes=[pltpu.VMEM((64, 128), jnp.float32)],
        compiler_params=limit(8),
        name="score",
    )(slices, near, far)


def to_core(value):
    return lax.ppermute(value, "tensor", [(t, t ^ 1) for t in range(16)])


def per_device(acts, grads, proj_in, proj_out, queries):
    length = acts.shape[1]
    rank = proj_in.shape[1]
    pin, pout = proj_in.T, proj_out.T

    with jax.named_scope("sides"):
        other, queries = project(False, acts, grads, pin, pout, queries)
        beside = lax.ppermute(queries, "dp", [(d, d ^ 1) for d in range(8)])
        got = to_core(other)
        (own,) = project(True, acts, grads, pin, pout)
        total, pair = merge(own, got, queries, beside)
        sides = lax.all_to_all(total, "tensor", 0, 0, tiled=True, axis_index_groups=CHIPS)

    with jax.named_scope("queries"):
        blocks = [pair] + [
            lax.ppermute(pair, "dp", [(d, (d + 2 * dy) % 8) for d in range(8)]) for dy in (1, 2, 3)
        ]

    with jax.named_scope("encode"):
        encoded, near = encode(sides, *blocks)
        slices = lax.all_to_all(encoded, "tensor", 0, 0, tiled=True)
        far = to_core(near)

    with jax.named_scope("scores"):
        part = score(length ** (-0.5) / rank, slices, near, far)
        parts = lax.all_to_all(part, "tensor", 0, 0, tiled=True, axis_index_groups=CHIPS)
        return jnp.sum(parts, axis=0)


def solution(mesh):
    in_specs = (
        P("dp", None, "tensor"),
        P("dp", None, "tensor"),
        P("tensor", None),
        P("tensor", None),
        P("dp", "tensor"),
    )
    out_specs = P("dp", None)
    return jax.shard_map(
        per_device, mesh=mesh, in_specs=in_specs, out_specs=out_specs, check_vma=False
    )
```

```python
import functools

import jax
import jax.numpy as jnp
from jax import lax
from jax.experimental import pallas as pl
from jax.experimental.pallas import tpu as pltpu
from jax.sharding import PartitionSpec as P

NT = (((1,), (1,)), ((), ()))
CHIPS = [[c + 2 * chip for chip in range(8)] for c in range(2)]
AHEAD = 4
HBM = pl.BlockSpec(memory_space=pltpu.HBM)
VMEM = pl.BlockSpec(memory_space=pltpu.VMEM)


def in_hbm(value):
    return pltpu.with_memory_space_constraint(value, pltpu.HBM)


def limit(mib):
    return pltpu.CompilerParams(vmem_limit_bytes=mib << 20)


def shape(*dims):
    return jax.ShapeDtypeStruct(dims, jnp.float32)


def project_kernel(mine, ahead, acts, grads, *rest):
    if mine:
        held_pin, held_pout, ahead_a, ahead_g, out, held_a, held_g, sem = rest
    else:
        pin, pout, queries, out, passed, held_pin, held_pout, ahead_a, ahead_g, held_a, held_g, sem, p_sem = rest
    examples, rank, rows = out.shape[0], out.shape[1] // 2, out.shape[2]
    core = lax.axis_index("tensor") % 2
    part = core if mine else 1 - core

    def fetch(e, part, to_a, to_g, slot):
        here = pl.ds(pl.multiple_of(part * rows, rows), rows)
        to = pl.ds(slot * rows, rows)
        return [
            pltpu.make_async_copy(grads.at[e, here, :], to_g.at[to, :], sem.at[0, e]),
            pltpu.make_async_copy(acts.at[e, here, :], to_a.at[to, :], sem.at[1, e]),
        ]

    skip = ahead if mine else 0
    blocks = [fetch(e, part, held_a, held_g, e - skip) for e in range(skip, examples)]
    if mine:
        for block in blocks:
            for copy in block:
                copy.start()
    else:
        weights = [
            pltpu.make_async_copy(pout, held_pout, p_sem.at[0]),
            pltpu.make_async_copy(pin, held_pin, p_sem.at[1]),
        ]
        for copy in weights + blocks[0] + blocks[1]:
            copy.start()
        for copy in weights:
            copy.wait()
        for block in blocks[2:]:
            for copy in block:
                copy.start()

    def multiply(e, from_a, from_g, slot):
        at = pl.ds(slot * rows, 2 * rows)
        so = lax.dot_general(held_pout[...], from_g[at, :], NT, preferred_element_type=jnp.float32)
        si = lax.dot_general(held_pin[...], from_a[at, :], NT, preferred_element_type=jnp.float32)
        for k in range(2):
            out[e + k, :rank, :] = so[:, k * rows : (k + 1) * rows]
            out[e + k, rank:, :] = si[:, k * rows : (k + 1) * rows]

    if mine:
        for e in range(0, ahead, 2):
            multiply(e, ahead_a, ahead_g, e)
    later = []
    for e in range(skip, examples, 2):
        for copy in blocks[e - skip] + blocks[e + 1 - skip]:
            copy.wait()
        if not mine and e == 2:
            later = [pltpu.make_async_copy(queries, passed, p_sem.at[2])]
            for k in range(ahead):
                to = pl.ds(k * rows, rows)
                here = pl.ds(pl.multiple_of(core * rows, rows), rows)
                later.append(pltpu.make_async_copy(grads.at[k, here, :], ahead_g.at[to, :], sem.at[2, k]))
                later.append(pltpu.make_async_copy(acts.at[k, here, :], ahead_a.at[to, :], sem.at[3, k]))
            for copy in later:
                copy.start()
        multiply(e, held_a, held_g, e - skip)
    for copy in later:
        copy.wait()


def project(mine, ahead, acts, grads, *more):
    examples, length, width_in = acts.shape
    width_out = grads.shape[2]
    rows = length // 2
    kept = (examples - ahead if mine else examples) * rows
    out_shape = [pltpu.VMEM((examples, 2 * more[0].shape[0], rows), jnp.float32)]
    scratch_shapes = [
        pltpu.VMEM((kept, width_in), acts.dtype),
        pltpu.VMEM((kept, width_out), grads.dtype),
        pltpu.SemaphoreType.DMA((4, examples)),
    ]
    if not mine:
        pin, pout, queries = more
        out_shape += [pltpu.VMEM(v.shape, v.dtype) for v in (queries, pin, pout)]
        out_shape += [pltpu.VMEM((ahead * rows, v.shape[2]), v.dtype) for v in (acts, grads)]
        scratch_shapes.append(pltpu.SemaphoreType.DMA((3,)))
        more = [in_hbm(v) for v in more]
    return pl.pallas_call(
        functools.partial(project_kernel, mine, ahead),
        out_shape=out_shape,
        in_specs=[HBM] * 2 + [VMEM if mine else HBM] * len(more),
        out_specs=[VMEM] * len(out_shape),
        scratch_shapes=scratch_shapes,
        compiler_params=limit(24),
        name="project_own" if mine else "project_other",
    )(in_hbm(acts), in_hbm(grads), *more)


def merge_kernel(own, got, queries, beside, total, pair):
    total[...] = own[...] + got[...]
    n = queries.shape[0]
    x_hi = lax.axis_index("dp") % 2
    pair[pl.ds(pl.multiple_of(x_hi * n, n), n), :] = queries[...]
    pair[pl.ds(pl.multiple_of((1 - x_hi) * n, n), n), :] = beside[...]


def merge(own, got, queries, beside):
    n, k = queries.shape
    return pl.pallas_call(
        merge_kernel,
        out_shape=[pltpu.VMEM(own.shape, jnp.float32), pltpu.VMEM((2 * n, k), jnp.float32)],
        in_specs=[VMEM] * 4,
        out_specs=[VMEM] * 2,
        compiler_params=limit(8),
        name="merge",
    )(own, got, queries, beside)


def encode_kernel(sides, q0, q1, q2, q3, out, near):
    for dy, block in enumerate((q0, q1, q2, q3)):
        near[pl.ds(dy * block.shape[0], block.shape[0]), :] = block[...]
    total = ((sides[0] + sides[1]) + (sides[2] + sides[3])) + ((sides[4] + sides[5]) + (sides[6] + sides[7]))
    rank = total.shape[0] // 2
    enc = lax.dot_general(
        total[:rank], total[rank:], NT, precision=lax.Precision.HIGHEST, preferred_element_type=jnp.float32
    )
    out[...] = jnp.zeros_like(out)
    for t in range(16):
        out[t, :, :rank] = enc[8 * (t // 2) : 8 * (t // 2) + 8, :]


def encode(sides, *blocks):
    n, k = blocks[0].shape
    return pl.pallas_call(
        encode_kernel,
        out_shape=[shape(16, 8, 128), shape(4 * n, k)],
        in_specs=[VMEM] * 5,
        out_specs=[VMEM] * 2,
        compiler_params=limit(8),
        name="encode",
    )(sides, *blocks)


def score_kernel(scale, slices, near, far, out, tiles):
    core = lax.axis_index("tensor") % 2
    y = lax.axis_index("dp") // 2
    for e in range(8):
        tiles[pl.ds(8 * e, 8), :] = slices[2 * e] + slices[2 * e + 1]
    rows = [tiles[pl.ds(i, 8, stride=8), :][:, :64] for i in range(8)]
    low, high = jnp.concatenate(rows[:4], axis=1), jnp.concatenate(rows[4:], axis=1)
    mine = jnp.where(core == 0, low, high) * scale
    theirs = jnp.where(core == 0, high, low) * scale

    def halves(value):
        high = value.astype(jnp.bfloat16)
        return high, (value - high.astype(jnp.float32)).astype(jnp.bfloat16)

    def dot(enc, block):
        (a, b), (c, d) = halves(enc), halves(block[...])
        both = jnp.concatenate([a, b], axis=0)
        by_high = lax.dot_general(both, c, NT, preferred_element_type=jnp.float32)
        by_low = lax.dot_general(both, d, NT, preferred_element_type=jnp.float32)
        return by_high[:8] + (by_high[8:] + by_low[:8] + by_low[8:])

    part = dot(mine, near) + dot(theirs, far)
    for dy in range(4):
        columns = pl.ds(pl.multiple_of((y - dy + 4) % 4 * 128, 128), 128)
        for g in range(8):
            out[g, :, columns] = part[:, 128 * dy : 128 * dy + 128]


def score(scale, slices, near, far):
    return pl.pallas_call(
        functools.partial(score_kernel, scale),
        out_shape=shape(8, 8, 512),
        in_specs=[VMEM] * 3,
        out_specs=VMEM,
        scratch_shapes=[pltpu.VMEM((64, 128), jnp.float32)],
        compiler_params=limit(8),
        name="score",
    )(slices, near, far)


def to_core(value):
    return lax.ppermute(value, "tensor", [(t, t ^ 1) for t in range(16)])


def per_device(acts, grads, proj_in, proj_out, queries):
    length = acts.shape[1]
    rank = proj_in.shape[1]
    pin, pout = proj_in.T, proj_out.T

    with jax.named_scope("sides"):
        other, queries, *first = project(False, AHEAD, acts, grads, pin, pout, queries)
        beside = lax.ppermute(queries, "dp", [(d, d ^ 1) for d in range(8)])
        got = to_core(other)
        (own,) = project(True, AHEAD, acts, grads, *first)
        total, pair = merge(own, got, queries, beside)
        sides = lax.all_to_all(total, "tensor", 0, 0, tiled=True, axis_index_groups=CHIPS)

    with jax.named_scope("queries"):
        blocks = [pair] + [
            lax.ppermute(pair, "dp", [(d, (d + 2 * dy) % 8) for d in range(8)]) for dy in (1, 2, 3)
        ]

    with jax.named_scope("encode"):
        encoded, near = encode(sides, *blocks)
        slices = lax.all_to_all(encoded, "tensor", 0, 0, tiled=True)
        far = to_core(near)

    with jax.named_scope("scores"):
        part = score(length ** (-0.5) / rank, slices, near, far)
        parts = lax.all_to_all(part, "tensor", 0, 0, tiled=True, axis_index_groups=CHIPS)
        return jnp.sum(parts, axis=0)


def solution(mesh):
    in_specs = (
        P("dp", None, "tensor"),
        P("dp", None, "tensor"),
        P("tensor", None),
        P("tensor", None),
        P("dp", "tensor"),
    )
    out_specs = P("dp", None)
    return jax.shard_map(
        per_device, mesh=mesh, in_specs=in_specs, out_specs=out_specs, check_vma=False
    )
```

```python
import functools

import jax
import jax.numpy as jnp
from jax import lax
from jax.experimental import pallas as pl
from jax.experimental.pallas import tpu as pltpu
from jax.sharding import PartitionSpec as P

NT = (((1,), (1,)), ((), ()))
CHIPS = [[c + 2 * chip for chip in range(8)] for c in range(2)]
AHEAD = 4
HBM = pl.BlockSpec(memory_space=pltpu.HBM)
VMEM = pl.BlockSpec(memory_space=pltpu.VMEM)


def in_hbm(value):
    return pltpu.with_memory_space_constraint(value, pltpu.HBM)


def limit(mib):
    return pltpu.CompilerParams(vmem_limit_bytes=mib << 20)


def shape(*dims):
    return jax.ShapeDtypeStruct(dims, jnp.float32)


def project_kernel(mine, ahead, acts, grads, *rest):
    if mine:
        held_pin, held_pout, ahead_a, ahead_g, out, held_a, held_g, sem = rest
    else:
        pin, pout, queries, out, passed, held_pin, held_pout, ahead_a, ahead_g, held_a, held_g, sem, p_sem = rest
    examples, rank, rows = out.shape[0], out.shape[1] // 2, out.shape[2]
    core = lax.axis_index("tensor") % 2
    part = core if mine else 1 - core

    def fetch(e, part, to_a, to_g, slot):
        here = pl.ds(pl.multiple_of(part * rows, rows), rows)
        to = pl.ds(slot * rows, rows)
        return [
            pltpu.make_async_copy(grads.at[e, here, :], to_g.at[to, :], sem.at[0, e]),
            pltpu.make_async_copy(acts.at[e, here, :], to_a.at[to, :], sem.at[1, e]),
        ]

    skip = ahead if mine else 0
    blocks = [fetch(e, part, held_a, held_g, e - skip) for e in range(skip, examples)]
    if mine:
        for block in blocks:
            for copy in block:
                copy.start()
    else:
        weights = [
            pltpu.make_async_copy(pout, held_pout, p_sem.at[0]),
            pltpu.make_async_copy(pin, held_pin, p_sem.at[1]),
        ]
        for copy in weights + blocks[0] + blocks[1]:
            copy.start()
        for copy in weights:
            copy.wait()
        for block in blocks[2:]:
            for copy in block:
                copy.start()

    def push(e, accs, from_a, from_g, slot):
        step = 0
        for rows_in, weights, which in ((from_g, held_pout, 0), (from_a, held_pin, 1)):
            for k in range(weights.shape[1] // 256):
                cut = slice(256 * k, 256 * k + 256)
                for unit in range(2):
                    block = rows_in[pl.ds((slot + unit) * rows, rows), cut]
                    pltpu.matmul_push_rhs(block, step % 2, unit, transpose=True)
                    pltpu.matmul_acc_lhs(accs[2 * unit + which], weights[:, cut], load_staged_rhs=step % 2)
                step += 1

    def pop(e, accs):
        for unit in range(2):
            out[e + unit, :rank, :] = pltpu.matmul_pop(accs[2 * unit])
            out[e + unit, rank:, :] = pltpu.matmul_pop(accs[2 * unit + 1])

    def body(*accs):
        later = []
        for e in range(0, examples, 2):
            turn = accs[4 * (e // 2 % 2) :][:4]
            if e < skip:
                push(e, turn, ahead_a, ahead_g, e)
            else:
                for copy in blocks[e - skip] + blocks[e + 1 - skip]:
                    copy.wait()
                if not mine and not later:
                    later = [pltpu.make_async_copy(queries, passed, p_sem.at[2])]
                    for k in range(ahead):
                        to = pl.ds(k * rows, rows)
                        here = pl.ds(pl.multiple_of(core * rows, rows), rows)
                        later.append(pltpu.make_async_copy(grads.at[k, here, :], ahead_g.at[to, :], sem.at[2, k]))
                        later.append(pltpu.make_async_copy(acts.at[k, here, :], ahead_a.at[to, :], sem.at[3, k]))
                    for copy in later:
                        copy.start()
                push(e, turn, held_a, held_g, e - skip)
            if e >= 2:
                pop(e - 2, accs[4 * ((e - 2) // 2 % 2) :][:4])
        pop(examples - 2, accs[4 * ((examples - 2) // 2 % 2) :][:4])
        for copy in later:
            copy.wait()

    units = [pltpu.ACC(unit)((rank, rows), jnp.float32) for _ in range(2) for unit in (0, 0, 1, 1)]
    pl.run_scoped(body, *units)


def project(mine, ahead, acts, grads, *more):
    examples, length, width_in = acts.shape
    width_out = grads.shape[2]
    rows = length // 2
    kept = (examples - ahead if mine else examples) * rows
    out_shape = [pltpu.VMEM((examples, 2 * more[0].shape[0], rows), jnp.float32)]
    scratch_shapes = [
        pltpu.VMEM((kept, width_in), acts.dtype),
        pltpu.VMEM((kept, width_out), grads.dtype),
        pltpu.SemaphoreType.DMA((4, examples)),
    ]
    if not mine:
        pin, pout, queries = more
        out_shape += [pltpu.VMEM(v.shape, v.dtype) for v in (queries, pin, pout)]
        out_shape += [pltpu.VMEM((ahead * rows, v.shape[2]), v.dtype) for v in (acts, grads)]
        scratch_shapes.append(pltpu.SemaphoreType.DMA((3,)))
        more = [in_hbm(v) for v in more]
    return pl.pallas_call(
        functools.partial(project_kernel, mine, ahead),
        out_shape=out_shape,
        in_specs=[HBM] * 2 + [VMEM if mine else HBM] * len(more),
        out_specs=[VMEM] * len(out_shape),
        scratch_shapes=scratch_shapes,
        compiler_params=limit(24),
        name="project_own" if mine else "project_other",
    )(in_hbm(acts), in_hbm(grads), *more)


def merge_kernel(own, got, queries, beside, total, pair):
    total[...] = own[...] + got[...]
    n = queries.shape[0]
    x_hi = lax.axis_index("dp") % 2
    pair[pl.ds(pl.multiple_of(x_hi * n, n), n), :] = queries[...]
    pair[pl.ds(pl.multiple_of((1 - x_hi) * n, n), n), :] = beside[...]


def merge(own, got, queries, beside):
    n, k = queries.shape
    return pl.pallas_call(
        merge_kernel,
        out_shape=[pltpu.VMEM(own.shape, jnp.float32), pltpu.VMEM((2 * n, k), jnp.float32)],
        in_specs=[VMEM] * 4,
        out_specs=[VMEM] * 2,
        compiler_params=limit(8),
        name="merge",
    )(own, got, queries, beside)


def encode_kernel(sides, q0, q1, q2, q3, out, near):
    for dy, block in enumerate((q0, q1, q2, q3)):
        near[pl.ds(dy * block.shape[0], block.shape[0]), :] = block[...]
    total = ((sides[0] + sides[1]) + (sides[2] + sides[3])) + ((sides[4] + sides[5]) + (sides[6] + sides[7]))
    rank = total.shape[0] // 2
    enc = lax.dot_general(
        total[:rank], total[rank:], NT, precision=lax.Precision.HIGHEST, preferred_element_type=jnp.float32
    )
    out[...] = jnp.zeros_like(out)
    for t in range(16):
        out[t, :, :rank] = enc[8 * (t // 2) : 8 * (t // 2) + 8, :]


def encode(sides, *blocks):
    n, k = blocks[0].shape
    return pl.pallas_call(
        encode_kernel,
        out_shape=[shape(16, 8, 128), shape(4 * n, k)],
        in_specs=[VMEM] * 5,
        out_specs=[VMEM] * 2,
        compiler_params=limit(8),
        name="encode",
    )(sides, *blocks)


def score_kernel(scale, slices, near, far, out, tiles):
    core = lax.axis_index("tensor") % 2
    y = lax.axis_index("dp") // 2
    for e in range(8):
        tiles[pl.ds(8 * e, 8), :] = slices[2 * e] + slices[2 * e + 1]
    rows = [tiles[pl.ds(i, 8, stride=8), :][:, :64] for i in range(8)]
    low, high = jnp.concatenate(rows[:4], axis=1), jnp.concatenate(rows[4:], axis=1)
    mine = jnp.where(core == 0, low, high) * scale
    theirs = jnp.where(core == 0, high, low) * scale

    def halves(value):
        high = value.astype(jnp.bfloat16)
        return high, (value - high.astype(jnp.float32)).astype(jnp.bfloat16)

    def dot(enc, block):
        (a, b), (c, d) = halves(enc), halves(block[...])
        both = jnp.concatenate([a, b], axis=0)
        by_high = lax.dot_general(both, c, NT, preferred_element_type=jnp.float32)
        by_low = lax.dot_general(both, d, NT, preferred_element_type=jnp.float32)
        return by_high[:8] + (by_high[8:] + by_low[:8] + by_low[8:])

    part = dot(mine, near) + dot(theirs, far)
    for dy in range(4):
        columns = pl.ds(pl.multiple_of((y - dy + 4) % 4 * 128, 128), 128)
        for g in range(8):
            out[g, :, columns] = part[:, 128 * dy : 128 * dy + 128]


def score(scale, slices, near, far):
    return pl.pallas_call(
        functools.partial(score_kernel, scale),
        out_shape=shape(8, 8, 512),
        in_specs=[VMEM] * 3,
        out_specs=VMEM,
        scratch_shapes=[pltpu.VMEM((64, 128), jnp.float32)],
        compiler_params=limit(8),
        name="score",
    )(slices, near, far)


def to_core(value):
    return lax.ppermute(value, "tensor", [(t, t ^ 1) for t in range(16)])


def per_device(acts, grads, proj_in, proj_out, queries):
    length = acts.shape[1]
    rank = proj_in.shape[1]
    pin, pout = proj_in.T, proj_out.T

    with jax.named_scope("sides"):
        other, queries, *first = project(False, AHEAD, acts, grads, pin, pout, queries)
        beside = lax.ppermute(queries, "dp", [(d, d ^ 1) for d in range(8)])
        got = to_core(other)
        (own,) = project(True, AHEAD, acts, grads, *first)
        total, pair = merge(own, got, queries, beside)
        sides = lax.all_to_all(total, "tensor", 0, 0, tiled=True, axis_index_groups=CHIPS)

    with jax.named_scope("queries"):
        blocks = [pair] + [
            lax.ppermute(pair, "dp", [(d, (d + 2 * dy) % 8) for d in range(8)]) for dy in (1, 2, 3)
        ]

    with jax.named_scope("encode"):
        encoded, near = encode(sides, *blocks)
        slices = lax.all_to_all(encoded, "tensor", 0, 0, tiled=True)
        far = to_core(near)

    with jax.named_scope("scores"):
        part = score(length ** (-0.5) / rank, slices, near, far)
        parts = lax.all_to_all(part, "tensor", 0, 0, tiled=True, axis_index_groups=CHIPS)
        return jnp.sum(parts, axis=0)


def solution(mesh):
    in_specs = (
        P("dp", None, "tensor"),
        P("dp", None, "tensor"),
        P("tensor", None),
        P("tensor", None),
        P("dp", "tensor"),
    )
    out_specs = P("dp", None)
    return jax.shard_map(
        per_device, mesh=mesh, in_specs=in_specs, out_specs=out_specs, check_vma=False
    )
```

```python
import functools

import jax
import jax.numpy as jnp
from jax import lax
from jax.experimental import pallas as pl
from jax.experimental.pallas import tpu as pltpu
from jax.sharding import PartitionSpec as P

NT = (((1,), (1,)), ((), ()))
CHIPS = [[c + 2 * chip for chip in range(8)] for c in range(2)]
AHEAD = 2
HBM = pl.BlockSpec(memory_space=pltpu.HBM)
VMEM = pl.BlockSpec(memory_space=pltpu.VMEM)


def in_hbm(value):
    return pltpu.with_memory_space_constraint(value, pltpu.HBM)


def limit(mib):
    return pltpu.CompilerParams(vmem_limit_bytes=mib << 20)


def shape(*dims):
    return jax.ShapeDtypeStruct(dims, jnp.float32)


def project_kernel(mine, ahead, acts, grads, *rest):
    if mine:
        held_pin, held_pout, ahead_a, ahead_g, out, held_a, held_g, sem = rest
    else:
        pin, pout, queries, out, passed, held_pin, held_pout, ahead_a, ahead_g, held_a, held_g, sem, p_sem = rest
    examples, rank, rows = out.shape[0], out.shape[1] // 2, out.shape[2]
    core = lax.axis_index("tensor") % 2
    part = core if mine else 1 - core

    def fetch(e, part, to_a, to_g, slot):
        here = pl.ds(pl.multiple_of(part * rows, rows), rows)
        to = pl.ds(slot * rows, rows)
        return [
            pltpu.make_async_copy(grads.at[e, here, :], to_g.at[to, :], sem.at[0, e]),
            pltpu.make_async_copy(acts.at[e, here, :], to_a.at[to, :], sem.at[1, e]),
        ]

    skip = ahead if mine else 0
    blocks = [fetch(e, part, held_a, held_g, e - skip) for e in range(skip, examples)]
    if mine:
        for block in blocks:
            for copy in block:
                copy.start()
    else:
        weights = [
            pltpu.make_async_copy(pout, held_pout, p_sem.at[0]),
            pltpu.make_async_copy(pin, held_pin, p_sem.at[1]),
        ]
        for copy in weights + blocks[0] + blocks[1]:
            copy.start()
        for copy in weights:
            copy.wait()
        for block in blocks[2:4]:
            for copy in block:
                copy.start()

    def push(e, accs, from_a, from_g, slot):
        step = 0
        for rows_in, weights, which in ((from_g, held_pout, 0), (from_a, held_pin, 1)):
            for k in range(weights.shape[1] // 256):
                cut = slice(256 * k, 256 * k + 256)
                for unit in range(2):
                    block = rows_in[pl.ds((slot + unit) * rows, rows), cut]
                    pltpu.matmul_push_rhs(block, step % 2, unit, transpose=True)
                    pltpu.matmul_acc_lhs(accs[2 * unit + which], weights[:, cut], load_staged_rhs=step % 2)
                step += 1

    def pop(e, accs):
        for unit in range(2):
            out[e + unit, :rank, :] = pltpu.matmul_pop(accs[2 * unit])
            out[e + unit, rank:, :] = pltpu.matmul_pop(accs[2 * unit + 1])

    def body(*accs):
        later = []
        for e in range(0, examples, 2):
            turn = accs[4 * (e // 2 % 2) :][:4]
            if e < skip:
                push(e, turn, ahead_a, ahead_g, e)
            else:
                for copy in blocks[e - skip] + blocks[e + 1 - skip]:
                    copy.wait()
                if not mine:
                    for block in blocks[e + 4 : e + 4 + 2]:
                        for copy in block:
                            copy.start()
                if not mine and e + 4 + 2 >= examples and not later:
                    later = [pltpu.make_async_copy(queries, passed, p_sem.at[2])]
                    for k in range(ahead):
                        to = pl.ds(k * rows, rows)
                        here = pl.ds(pl.multiple_of(core * rows, rows), rows)
                        later.append(pltpu.make_async_copy(grads.at[k, here, :], ahead_g.at[to, :], sem.at[2, k]))
                        later.append(pltpu.make_async_copy(acts.at[k, here, :], ahead_a.at[to, :], sem.at[3, k]))
                    for copy in later:
                        copy.start()
                push(e, turn, held_a, held_g, e - skip)
            if e >= 2:
                pop(e - 2, accs[4 * ((e - 2) // 2 % 2) :][:4])
        pop(examples - 2, accs[4 * ((examples - 2) // 2 % 2) :][:4])
        for copy in later:
            copy.wait()

    units = [pltpu.ACC(unit)((rank, rows), jnp.float32) for _ in range(2) for unit in (0, 0, 1, 1)]
    pl.run_scoped(body, *units)


def project(mine, ahead, acts, grads, *more):
    examples, length, width_in = acts.shape
    width_out = grads.shape[2]
    rows = length // 2
    kept = (examples - ahead if mine else examples) * rows
    out_shape = [pltpu.VMEM((examples, 2 * more[0].shape[0], rows), jnp.float32)]
    scratch_shapes = [
        pltpu.VMEM((kept, width_in), acts.dtype),
        pltpu.VMEM((kept, width_out), grads.dtype),
        pltpu.SemaphoreType.DMA((4, examples)),
    ]
    if not mine:
        pin, pout, queries = more
        out_shape += [pltpu.VMEM(v.shape, v.dtype) for v in (queries, pin, pout)]
        out_shape += [pltpu.VMEM((ahead * rows, v.shape[2]), v.dtype) for v in (acts, grads)]
        scratch_shapes.append(pltpu.SemaphoreType.DMA((3,)))
        more = [in_hbm(v) for v in more]
    return pl.pallas_call(
        functools.partial(project_kernel, mine, ahead),
        out_shape=out_shape,
        in_specs=[HBM] * 2 + [VMEM if mine else HBM] * len(more),
        out_specs=[VMEM] * len(out_shape),
        scratch_shapes=scratch_shapes,
        compiler_params=limit(24),
        name="project_own" if mine else "project_other",
    )(in_hbm(acts), in_hbm(grads), *more)


def merge_kernel(own, got, queries, beside, total, pair):
    total[...] = own[...] + got[...]
    n = queries.shape[0]
    x_hi = lax.axis_index("dp") % 2
    pair[pl.ds(pl.multiple_of(x_hi * n, n), n), :] = queries[...]
    pair[pl.ds(pl.multiple_of((1 - x_hi) * n, n), n), :] = beside[...]


def merge(own, got, queries, beside):
    n, k = queries.shape
    return pl.pallas_call(
        merge_kernel,
        out_shape=[pltpu.VMEM(own.shape, jnp.float32), pltpu.VMEM((2 * n, k), jnp.float32)],
        in_specs=[VMEM] * 4,
        out_specs=[VMEM] * 2,
        compiler_params=limit(8),
        name="merge",
    )(own, got, queries, beside)


def encode_kernel(sides, q0, q1, q2, q3, out, near):
    for dy, block in enumerate((q0, q1, q2, q3)):
        near[pl.ds(dy * block.shape[0], block.shape[0]), :] = block[...]
    total = ((sides[0] + sides[1]) + (sides[2] + sides[3])) + ((sides[4] + sides[5]) + (sides[6] + sides[7]))
    rank = total.shape[0] // 2
    enc = lax.dot_general(
        total[:rank], total[rank:], NT, precision=lax.Precision.HIGHEST, preferred_element_type=jnp.float32
    )
    out[...] = jnp.zeros_like(out)
    for t in range(16):
        out[t, :, :rank] = enc[8 * (t // 2) : 8 * (t // 2) + 8, :]


def encode(sides, *blocks):
    n, k = blocks[0].shape
    return pl.pallas_call(
        encode_kernel,
        out_shape=[shape(16, 8, 128), shape(4 * n, k)],
        in_specs=[VMEM] * 5,
        out_specs=[VMEM] * 2,
        compiler_params=limit(8),
        name="encode",
    )(sides, *blocks)


def score_kernel(scale, slices, near, far, out, tiles):
    core = lax.axis_index("tensor") % 2
    y = lax.axis_index("dp") // 2
    for e in range(8):
        tiles[pl.ds(8 * e, 8), :] = slices[2 * e] + slices[2 * e + 1]
    rows = [tiles[pl.ds(i, 8, stride=8), :][:, :64] for i in range(8)]
    low, high = jnp.concatenate(rows[:4], axis=1), jnp.concatenate(rows[4:], axis=1)
    mine = jnp.where(core == 0, low, high) * scale
    theirs = jnp.where(core == 0, high, low) * scale

    def halves(value):
        high = value.astype(jnp.bfloat16)
        return high, (value - high.astype(jnp.float32)).astype(jnp.bfloat16)

    def dot(enc, block):
        (a, b), (c, d) = halves(enc), halves(block[...])
        both = jnp.concatenate([a, b], axis=0)
        by_high = lax.dot_general(both, c, NT, preferred_element_type=jnp.float32)
        by_low = lax.dot_general(both, d, NT, preferred_element_type=jnp.float32)
        return by_high[:8] + (by_high[8:] + by_low[:8] + by_low[8:])

    part = dot(mine, near) + dot(theirs, far)
    for dy in range(4):
        columns = pl.ds(pl.multiple_of((y - dy + 4) % 4 * 128, 128), 128)
        for g in range(8):
            out[g, :, columns] = part[:, 128 * dy : 128 * dy + 128]


def score(scale, slices, near, far):
    return pl.pallas_call(
        functools.partial(score_kernel, scale),
        out_shape=shape(8, 8, 512),
        in_specs=[VMEM] * 3,
        out_specs=VMEM,
        scratch_shapes=[pltpu.VMEM((64, 128), jnp.float32)],
        compiler_params=limit(8),
        name="score",
    )(slices, near, far)


def to_core(value):
    return lax.ppermute(value, "tensor", [(t, t ^ 1) for t in range(16)])


def per_device(acts, grads, proj_in, proj_out, queries):
    length = acts.shape[1]
    rank = proj_in.shape[1]
    pin, pout = proj_in.T, proj_out.T

    with jax.named_scope("sides"):
        other, queries, *first = project(False, AHEAD, acts, grads, pin, pout, queries)
        beside = lax.ppermute(queries, "dp", [(d, d ^ 1) for d in range(8)])
        got = to_core(other)
        (own,) = project(True, AHEAD, acts, grads, *first)
        total, pair = merge(own, got, queries, beside)
        sides = lax.all_to_all(total, "tensor", 0, 0, tiled=True, axis_index_groups=CHIPS)

    with jax.named_scope("queries"):
        blocks = [pair] + [
            lax.ppermute(pair, "dp", [(d, (d + 2 * dy) % 8) for d in range(8)]) for dy in (1, 2, 3)
        ]

    with jax.named_scope("encode"):
        encoded, near = encode(sides, *blocks)
        slices = lax.all_to_all(encoded, "tensor", 0, 0, tiled=True)
        far = to_core(near)

    with jax.named_scope("scores"):
        part = score(length ** (-0.5) / rank, slices, near, far)
        parts = lax.all_to_all(part, "tensor", 0, 0, tiled=True, axis_index_groups=CHIPS)
        return jnp.sum(parts, axis=0)


def solution(mesh):
    in_specs = (
        P("dp", None, "tensor"),
        P("dp", None, "tensor"),
        P("tensor", None),
        P("tensor", None),
        P("dp", "tensor"),
    )
    out_specs = P("dp", None)
    return jax.shard_map(
        per_device, mesh=mesh, in_specs=in_specs, out_specs=out_specs, check_vma=False
    )
```

```python
import functools

import jax
import jax.numpy as jnp
from jax import lax
from jax.experimental import pallas as pl
from jax.experimental.pallas import tpu as pltpu
from jax.sharding import PartitionSpec as P

NT = (((1,), (1,)), ((), ()))
CHIPS = [[c + 2 * chip for chip in range(8)] for c in range(2)]
ALONG = (0, 1, 3, 2)
AHEAD = 2
HBM = pl.BlockSpec(memory_space=pltpu.HBM)
VMEM = pl.BlockSpec(memory_space=pltpu.VMEM)


def in_hbm(value):
    return pltpu.with_memory_space_constraint(value, pltpu.HBM)


def limit(mib):
    return pltpu.CompilerParams(vmem_limit_bytes=mib << 20)


def shape(*dims):
    return jax.ShapeDtypeStruct(dims, jnp.float32)


def project_kernel(mine, ahead, acts, grads, *rest):
    if mine:
        held_pin, held_pout, ahead_a, ahead_g, out, held_a, held_g, sem = rest
    else:
        pin, pout, queries, out, passed, held_pin, held_pout, ahead_a, ahead_g, held_a, held_g, sem, p_sem = rest
    examples, rank, rows = out.shape[0], out.shape[1] // 2, out.shape[2]
    t = lax.axis_index("tensor")
    core = t % 2
    part = core if mine else 1 - core

    def spot(u, part):
        return 2 * ((t // 4 + ALONG[u // 2]) % 4) + (t // 2 + part) % 2, pl.ds(u % 2 * rows, rows)

    def fetch(u, part, to_a, to_g, slot):
        e, here = spot(u, part)
        to = pl.ds(slot * rows, rows)
        return [
            pltpu.make_async_copy(grads.at[e, here, :], to_g.at[to, :], sem.at[0, u]),
            pltpu.make_async_copy(acts.at[e, here, :], to_a.at[to, :], sem.at[1, u]),
        ]

    skip = ahead if mine else 0
    blocks = [fetch(e, part, held_a, held_g, e - skip) for e in range(skip, examples)]
    if mine:
        for block in blocks:
            for copy in block:
                copy.start()
    else:
        weights = [
            pltpu.make_async_copy(pout, held_pout, p_sem.at[0]),
            pltpu.make_async_copy(pin, held_pin, p_sem.at[1]),
        ]
        for copy in weights + blocks[0] + blocks[1]:
            copy.start()
        for copy in weights:
            copy.wait()
        for block in blocks[2:4]:
            for copy in block:
                copy.start()

    def push(e, accs, from_a, from_g, slot):
        step = 0
        for rows_in, weights, which in ((from_g, held_pout, 0), (from_a, held_pin, 1)):
            for k in range(weights.shape[1] // 256):
                cut = slice(256 * k, 256 * k + 256)
                for unit in range(2):
                    block = rows_in[pl.ds((slot + unit) * rows, rows), cut]
                    pltpu.matmul_push_rhs(block, step % 2, unit, transpose=True)
                    pltpu.matmul_acc_lhs(accs[2 * unit + which], weights[:, cut], load_staged_rhs=step % 2)
                step += 1

    def pop(e, accs):
        for unit in range(2):
            out[e + unit, :rank, :] = pltpu.matmul_pop(accs[2 * unit])
            out[e + unit, rank:, :] = pltpu.matmul_pop(accs[2 * unit + 1])

    def body(*accs):
        later = []
        for e in range(0, examples, 2):
            turn = accs[4 * (e // 2 % 2) :][:4]
            if e < skip:
                push(e, turn, ahead_a, ahead_g, e)
            else:
                for copy in blocks[e - skip] + blocks[e + 1 - skip]:
                    copy.wait()
                if not mine:
                    for block in blocks[e + 4 : e + 4 + 2]:
                        for copy in block:
                            copy.start()
                if not mine and e + 4 + 2 >= examples and not later:
                    later = [pltpu.make_async_copy(queries, passed, p_sem.at[2])]
                    for k in range(ahead):
                        to = pl.ds(k * rows, rows)
                        at, here = spot(k, core)
                        later.append(pltpu.make_async_copy(grads.at[at, here, :], ahead_g.at[to, :], sem.at[2, k]))
                        later.append(pltpu.make_async_copy(acts.at[at, here, :], ahead_a.at[to, :], sem.at[3, k]))
                    for copy in later:
                        copy.start()
                push(e, turn, held_a, held_g, e - skip)
            if e >= 2:
                pop(e - 2, accs[4 * ((e - 2) // 2 % 2) :][:4])
        pop(examples - 2, accs[4 * ((examples - 2) // 2 % 2) :][:4])
        for copy in later:
            copy.wait()

    units = [pltpu.ACC(unit)((rank, rows), jnp.float32) for _ in range(2) for unit in (0, 0, 1, 1)]
    pl.run_scoped(body, *units)


def project(mine, ahead, acts, grads, *more):
    examples, length, width_in = acts.shape
    width_out = grads.shape[2]
    rows = length // 2
    kept = (examples - ahead if mine else examples) * rows
    out_shape = [pltpu.VMEM((examples, 2 * more[0].shape[0], rows), jnp.float32)]
    scratch_shapes = [
        pltpu.VMEM((kept, width_in), acts.dtype),
        pltpu.VMEM((kept, width_out), grads.dtype),
        pltpu.SemaphoreType.DMA((4, examples)),
    ]
    if not mine:
        pin, pout, queries = more
        out_shape += [pltpu.VMEM(v.shape, v.dtype) for v in (queries, pin, pout)]
        out_shape += [pltpu.VMEM((ahead * rows, v.shape[2]), v.dtype) for v in (acts, grads)]
        scratch_shapes.append(pltpu.SemaphoreType.DMA((3,)))
        more = [in_hbm(v) for v in more]
    return pl.pallas_call(
        functools.partial(project_kernel, mine, ahead),
        out_shape=out_shape,
        in_specs=[HBM] * 2 + [VMEM if mine else HBM] * len(more),
        out_specs=[VMEM] * len(out_shape),
        scratch_shapes=scratch_shapes,
        compiler_params=limit(24),
        name="project_own" if mine else "project_other",
    )(in_hbm(acts), in_hbm(grads), *more)


def merge_kernel(own, got, queries, beside, *outs):
    for k in range(4):
        outs[k][...] = own[2 * k : 2 * k + 2] + got[2 * k : 2 * k + 2]
    pair = outs[4]
    n = queries.shape[0]
    x_hi = lax.axis_index("dp") % 2
    pair[pl.ds(pl.multiple_of(x_hi * n, n), n), :] = queries[...]
    pair[pl.ds(pl.multiple_of((1 - x_hi) * n, n), n), :] = beside[...]


def merge(own, got, queries, beside):
    n, k = queries.shape
    return pl.pallas_call(
        merge_kernel,
        out_shape=[shape(2, *own.shape[1:])] * 4 + [shape(2 * n, k)],
        in_specs=[VMEM] * 4,
        out_specs=[VMEM] * 5,
        compiler_params=limit(8),
        name="merge",
    )(own, got, queries, beside)


def relay_kernel(arrived, pair, out):
    out[...] = pair[...]


def relay(arrived, pair):
    return pl.pallas_call(
        relay_kernel,
        out_shape=shape(*pair.shape),
        in_specs=[pl.BlockSpec(memory_space=pl.ANY), VMEM],
        out_specs=VMEM,
        compiler_params=limit(8),
        name="relay",
    )(arrived, pair)


def halve_kernel(a, b, c, d, keep, send):
    core = lax.axis_index("tensor") % 2
    keep[...] = (a[core] + d[core]) + (b[core] + c[core])
    send[...] = (a[1 - core] + d[1 - core]) + (b[1 - core] + c[1 - core])


def halve(*sides):
    return pl.pallas_call(
        halve_kernel,
        out_shape=[shape(*sides[0].shape[1:])] * 2,
        in_specs=[VMEM] * 4,
        out_specs=[VMEM] * 2,
        compiler_params=limit(8),
        name="halve",
    )(*sides)


def encode_kernel(keep, got, q0, q1, q2, q3, out, near):
    for dy, block in enumerate((q0, q1, q2, q3)):
        near[pl.ds(dy * block.shape[0], block.shape[0]), :] = block[...]
    total = keep[...] + got[...]
    rank = total.shape[0] // 2
    enc = lax.dot_general(
        total[:rank], total[rank:], NT, precision=lax.Precision.HIGHEST, preferred_element_type=jnp.float32
    )
    out[...] = jnp.zeros_like(out)
    for t in range(16):
        out[t, :, :rank] = enc[8 * (t // 2) : 8 * (t // 2) + 8, :]


def encode(keep, got, blocks):
    n, k = blocks[0].shape
    return pl.pallas_call(
        encode_kernel,
        out_shape=[shape(16, 8, 128), shape(4 * n, k)],
        in_specs=[VMEM] * 6,
        out_specs=[VMEM] * 2,
        compiler_params=limit(8),
        name="encode",
    )(keep, got, *blocks)


def score_kernel(scale, slices, near, far, out, tiles):
    core = lax.axis_index("tensor") % 2
    y = lax.axis_index("dp") // 2
    for e in range(8):
        tiles[pl.ds(8 * e, 8), :] = slices[2 * e] + slices[2 * e + 1]
    rows = [tiles[pl.ds(i, 8, stride=8), :][:, :64] for i in range(8)]
    low, high = jnp.concatenate(rows[:4], axis=1), jnp.concatenate(rows[4:], axis=1)
    mine = jnp.where(core == 0, low, high) * scale
    theirs = jnp.where(core == 0, high, low) * scale

    def halves(value):
        high = value.astype(jnp.bfloat16)
        return high, (value - high.astype(jnp.float32)).astype(jnp.bfloat16)

    def dot(enc, block):
        (a, b), (c, d) = halves(enc), halves(block[...])
        both = jnp.concatenate([a, b], axis=0)
        by_high = lax.dot_general(both, c, NT, preferred_element_type=jnp.float32)
        by_low = lax.dot_general(both, d, NT, preferred_element_type=jnp.float32)
        return by_high[:8] + (by_high[8:] + by_low[:8] + by_low[8:])

    part = dot(mine, near) + dot(theirs, far)
    for dy in range(4):
        columns = pl.ds(pl.multiple_of((y - dy + 4) % 4 * 128, 128), 128)
        for g in range(8):
            out[g, :, columns] = part[:, 128 * dy : 128 * dy + 128]


def score(scale, slices, near, far):
    return pl.pallas_call(
        functools.partial(score_kernel, scale),
        out_shape=shape(8, 8, 512),
        in_specs=[VMEM] * 3,
        out_specs=VMEM,
        scratch_shapes=[pltpu.VMEM((64, 128), jnp.float32)],
        compiler_params=limit(8),
        name="score",
    )(slices, near, far)


def to_core(value):
    return lax.ppermute(value, "tensor", [(t, t ^ 1) for t in range(16)])


def to_line(value, dz):
    def to(t):
        return (t + 4 * dz) % 16 ^ (2 * (t % 2))

    return lax.ppermute(value, "tensor", [(t, to(t)) for t in range(16)])


def per_device(acts, grads, proj_in, proj_out, queries):
    length = acts.shape[1]
    rank = proj_in.shape[1]
    pin, pout = proj_in.T, proj_out.T

    with jax.named_scope("sides"):
        other, queries, *first = project(False, AHEAD, acts, grads, pin, pout, queries)
        beside = lax.ppermute(queries, "dp", [(d, d ^ 1) for d in range(8)])
        got = to_core(other)
        (own,) = project(True, AHEAD, acts, grads, *first)
        *sides, pair = merge(own, got, queries, beside)
        sides = [to_line(v, dz) for v, dz in zip(sides, ALONG)]
        pair = relay(sides[0], pair)
        keep, send = halve(*sides)
        got = to_core(send)

    with jax.named_scope("queries"):
        blocks = [pair] + [
            lax.ppermute(pair, "dp", [(d, (d + 2 * dy) % 8) for d in range(8)]) for dy in (1, 2, 3)
        ]

    with jax.named_scope("encode"):
        encoded, near = encode(keep, got, blocks)
        slices = lax.all_to_all(encoded, "tensor", 0, 0, tiled=True)
        far = to_core(near)

    with jax.named_scope("scores"):
        part = score(length ** (-0.5) / rank, slices, near, far)
        parts = lax.all_to_all(part, "tensor", 0, 0, tiled=True, axis_index_groups=CHIPS)
        return jnp.sum(parts, axis=0)


def solution(mesh):
    in_specs = (
        P("dp", None, "tensor"),
        P("dp", None, "tensor"),
        P("tensor", None),
        P("tensor", None),
        P("dp", "tensor"),
    )
    out_specs = P("dp", None)
    return jax.shard_map(
        per_device, mesh=mesh, in_specs=in_specs, out_specs=out_specs, check_vma=False
    )
```

```python
import functools

import jax
import jax.numpy as jnp
from jax import lax
from jax.experimental import pallas as pl
from jax.experimental.pallas import tpu as pltpu
from jax.sharding import PartitionSpec as P

NT = (((1,), (1,)), ((), ()))
CHIPS = [[c + 2 * chip for chip in range(8)] for c in range(2)]
ALONG = (0, 1, 3, 2)
AHEAD = 2
HBM = pl.BlockSpec(memory_space=pltpu.HBM)
VMEM = pl.BlockSpec(memory_space=pltpu.VMEM)


def in_hbm(value):
    return pltpu.with_memory_space_constraint(value, pltpu.HBM)


def limit(mib):
    return pltpu.CompilerParams(vmem_limit_bytes=mib << 20)


def shape(*dims):
    return jax.ShapeDtypeStruct(dims, jnp.float32)


def project_kernel(mine, ahead, acts, grads, *rest):
    if mine:
        held_pin, held_pout, ahead_a, ahead_g, out, held_a, held_g, sem = rest
    else:
        pin, pout, queries, out, passed, held_pin, held_pout, ahead_a, ahead_g, held_a, held_g, sem, p_sem = rest
    examples, rank, rows = out.shape[0], out.shape[1] // 2, out.shape[2]
    t = lax.axis_index("tensor")
    core = t % 2
    part = core if mine else 1 - core

    def spot(u, part):
        return 2 * ((t // 4 + ALONG[u // 2]) % 4) + (t // 2 + part) % 2, pl.ds(u % 2 * rows, rows)

    def fetch(u, part, to_a, to_g, slot):
        e, here = spot(u, part)
        to = pl.ds(slot * rows, rows)
        return [
            pltpu.make_async_copy(grads.at[e, here, :], to_g.at[to, :], sem.at[0, u]),
            pltpu.make_async_copy(acts.at[e, here, :], to_a.at[to, :], sem.at[1, u]),
        ]

    skip = ahead if mine else 0
    blocks = [fetch(e, part, held_a, held_g, e - skip) for e in range(skip, examples)]
    if mine:
        for block in blocks:
            for copy in block:
                copy.start()
    else:
        weights = [
            pltpu.make_async_copy(pout, held_pout, p_sem.at[0]),
            pltpu.make_async_copy(pin, held_pin, p_sem.at[1]),
        ]
        for copy in weights + blocks[0] + blocks[1]:
            copy.start()
        for copy in weights:
            copy.wait()
        for block in blocks[2:4]:
            for copy in block:
                copy.start()

    def push(e, accs, from_a, from_g, slot):
        step = 0
        for rows_in, weights, which in ((from_g, held_pout, 0), (from_a, held_pin, 1)):
            for k in range(weights.shape[1] // 256):
                cut = slice(256 * k, 256 * k + 256)
                for unit in range(2):
                    block = rows_in[pl.ds((slot + unit) * rows, rows), cut]
                    pltpu.matmul_push_rhs(block, step % 2, unit, transpose=True)
                    pltpu.matmul_acc_lhs(accs[2 * unit + which], weights[:, cut], load_staged_rhs=step % 2)
                step += 1

    def pop(e, accs):
        for unit in range(2):
            out[e + unit, :rank, :] = pltpu.matmul_pop(accs[2 * unit])
            out[e + unit, rank:, :] = pltpu.matmul_pop(accs[2 * unit + 1])

    def body(*accs):
        later = []
        for e in range(0, examples, 2):
            turn = accs[4 * (e // 2 % 2) :][:4]
            if e < skip:
                push(e, turn, ahead_a, ahead_g, e)
            else:
                for copy in blocks[e - skip] + blocks[e + 1 - skip]:
                    copy.wait()
                if not mine:
                    for block in blocks[e + 4 : e + 4 + 2]:
                        for copy in block:
                            copy.start()
                if not mine and e + 4 + 2 >= examples and not later:
                    later = [pltpu.make_async_copy(queries, passed, p_sem.at[2])]
                    for k in range(ahead):
                        to = pl.ds(k * rows, rows)
                        at, here = spot(k, core)
                        later.append(pltpu.make_async_copy(grads.at[at, here, :], ahead_g.at[to, :], sem.at[2, k]))
                        later.append(pltpu.make_async_copy(acts.at[at, here, :], ahead_a.at[to, :], sem.at[3, k]))
                    for copy in later:
                        copy.start()
                push(e, turn, held_a, held_g, e - skip)
            if e >= 2:
                pop(e - 2, accs[4 * ((e - 2) // 2 % 2) :][:4])
        pop(examples - 2, accs[4 * ((examples - 2) // 2 % 2) :][:4])
        for copy in later:
            copy.wait()

    units = [pltpu.ACC(unit)((rank, rows), jnp.float32) for _ in range(2) for unit in (0, 0, 1, 1)]
    pl.run_scoped(body, *units)


def project(mine, ahead, acts, grads, *more):
    examples, length, width_in = acts.shape
    width_out = grads.shape[2]
    rows = length // 2
    kept = (examples - ahead if mine else examples) * rows
    out_shape = [pltpu.VMEM((examples, 2 * more[0].shape[0], rows), jnp.float32)]
    scratch_shapes = [
        pltpu.VMEM((kept, width_in), acts.dtype),
        pltpu.VMEM((kept, width_out), grads.dtype),
        pltpu.SemaphoreType.DMA((4, examples)),
    ]
    if not mine:
        pin, pout, queries = more
        out_shape += [pltpu.VMEM(v.shape, v.dtype) for v in (queries, pin, pout)]
        out_shape += [pltpu.VMEM((ahead * rows, v.shape[2]), v.dtype) for v in (acts, grads)]
        scratch_shapes.append(pltpu.SemaphoreType.DMA((3,)))
        more = [in_hbm(v) for v in more]
    return pl.pallas_call(
        functools.partial(project_kernel, mine, ahead),
        out_shape=out_shape,
        in_specs=[HBM] * 2 + [VMEM if mine else HBM] * len(more),
        out_specs=[VMEM] * len(out_shape),
        scratch_shapes=scratch_shapes,
        compiler_params=limit(24),
        name="project_own" if mine else "project_other",
    )(in_hbm(acts), in_hbm(grads), *more)


def merge_kernel(own, got, queries, beside, *outs):
    for k in range(4):
        outs[k][...] = own[2 * k : 2 * k + 2] + got[2 * k : 2 * k + 2]
    pair = outs[4]
    n = queries.shape[0]
    x_hi = lax.axis_index("dp") % 2
    pair[pl.ds(pl.multiple_of(x_hi * n, n), n), :] = queries[...]
    pair[pl.ds(pl.multiple_of((1 - x_hi) * n, n), n), :] = beside[...]


def merge(own, got, queries, beside):
    n, k = queries.shape
    return pl.pallas_call(
        merge_kernel,
        out_shape=[shape(2, *own.shape[1:])] * 4 + [shape(2 * n, k)],
        in_specs=[VMEM] * 4,
        out_specs=[VMEM] * 5,
        compiler_params=limit(8),
        name="merge",
    )(own, got, queries, beside)


def relay_kernel(arrived, pair, out):
    out[...] = pair[...]


def relay(arrived, pair):
    return pl.pallas_call(
        relay_kernel,
        out_shape=shape(*pair.shape),
        in_specs=[pl.BlockSpec(memory_space=pl.ANY), VMEM],
        out_specs=VMEM,
        compiler_params=limit(8),
        name="relay",
    )(arrived, pair)


def halve_kernel(a, b, c, d, keep, send):
    core = lax.axis_index("tensor") % 2
    keep[...] = (a[core] + d[core]) + (b[core] + c[core])
    send[...] = (a[1 - core] + d[1 - core]) + (b[1 - core] + c[1 - core])


def halve(*sides):
    return pl.pallas_call(
        halve_kernel,
        out_shape=[shape(*sides[0].shape[1:])] * 2,
        in_specs=[VMEM] * 4,
        out_specs=[VMEM] * 2,
        compiler_params=limit(8),
        name="halve",
    )(*sides)


def encode_kernel(keep, got, q0, q1, q2, q3, out, near):
    for dy, block in enumerate((q0, q1, q2, q3)):
        near[pl.ds(dy * block.shape[0], block.shape[0]), :] = block[...]
    total = keep[...] + got[...]
    rank = total.shape[0] // 2
    enc = lax.dot_general(
        total[:rank], total[rank:], NT, precision=lax.Precision.HIGHEST, preferred_element_type=jnp.float32
    )
    for t in range(16):
        g = 8 * (t // 2)
        out[t] = jnp.concatenate([enc[g : g + 4, :], enc[g + 4 : g + 8, :]], axis=1)


def encode(keep, got, blocks):
    n, k = blocks[0].shape
    return pl.pallas_call(
        encode_kernel,
        out_shape=[shape(16, 4, 128), shape(4 * n, k)],
        in_specs=[VMEM] * 6,
        out_specs=[VMEM] * 2,
        compiler_params=limit(8),
        name="encode",
    )(keep, got, *blocks)


def score_kernel(scale, slices, near, far, out, tiles):
    core = lax.axis_index("tensor") % 2
    y = lax.axis_index("dp") // 2
    for e in range(8):
        tiles[pl.ds(4 * e, 4), :] = slices[2 * e] + slices[2 * e + 1]
    rows = [tiles[pl.ds(i, 8, stride=4), :] for i in range(4)]
    low = jnp.concatenate([row[:, :64] for row in rows], axis=1)
    high = jnp.concatenate([row[:, 64:] for row in rows], axis=1)
    mine = jnp.where(core == 0, low, high) * scale
    theirs = jnp.where(core == 0, high, low) * scale

    def halves(value):
        high = value.astype(jnp.bfloat16)
        return high, (value - high.astype(jnp.float32)).astype(jnp.bfloat16)

    def dot(enc, block):
        (a, b), (c, d) = halves(enc), halves(block[...])
        both = jnp.concatenate([a, b], axis=0)
        by_high = lax.dot_general(both, c, NT, preferred_element_type=jnp.float32)
        by_low = lax.dot_general(both, d, NT, preferred_element_type=jnp.float32)
        return by_high[:8] + (by_high[8:] + by_low[:8] + by_low[8:])

    part = dot(mine, near) + dot(theirs, far)
    for dy in range(4):
        columns = pl.ds(pl.multiple_of((y - dy + 4) % 4 * 128, 128), 128)
        for g in range(8):
            out[g, :, columns] = part[:, 128 * dy : 128 * dy + 128]


def score(scale, slices, near, far):
    return pl.pallas_call(
        functools.partial(score_kernel, scale),
        out_shape=shape(8, 8, 512),
        in_specs=[VMEM] * 3,
        out_specs=VMEM,
        scratch_shapes=[pltpu.VMEM((32, 128), jnp.float32)],
        compiler_params=limit(8),
        name="score",
    )(slices, near, far)


def to_core(value):
    return lax.ppermute(value, "tensor", [(t, t ^ 1) for t in range(16)])


def to_line(value, dz):
    def to(t):
        return (t + 4 * dz) % 16 ^ (2 * (t % 2))

    return lax.ppermute(value, "tensor", [(t, to(t)) for t in range(16)])


def per_device(acts, grads, proj_in, proj_out, queries):
    length = acts.shape[1]
    rank = proj_in.shape[1]
    pin, pout = proj_in.T, proj_out.T

    with jax.named_scope("sides"):
        other, queries, *first = project(False, AHEAD, acts, grads, pin, pout, queries)
        beside = lax.ppermute(queries, "dp", [(d, d ^ 1) for d in range(8)])
        got = to_core(other)
        (own,) = project(True, AHEAD, acts, grads, *first)
        *sides, pair = merge(own, got, queries, beside)
        sides = [to_line(v, dz) for v, dz in zip(sides, ALONG)]
        pair = relay(sides[0], pair)
        keep, send = halve(*sides)
        got = to_core(send)

    with jax.named_scope("queries"):
        blocks = [pair] + [
            lax.ppermute(pair, "dp", [(d, (d + 2 * dy) % 8) for d in range(8)]) for dy in (1, 2, 3)
        ]

    with jax.named_scope("encode"):
        encoded, near = encode(keep, got, blocks)
        slices = lax.all_to_all(encoded, "tensor", 0, 0, tiled=True)
        far = to_core(near)

    with jax.named_scope("scores"):
        part = score(length ** (-0.5) / rank, slices, near, far)
        parts = lax.all_to_all(part, "tensor", 0, 0, tiled=True, axis_index_groups=CHIPS)
        return jnp.sum(parts, axis=0)


def solution(mesh):
    in_specs = (
        P("dp", None, "tensor"),
        P("dp", None, "tensor"),
        P("tensor", None),
        P("tensor", None),
        P("dp", "tensor"),
    )
    out_specs = P("dp", None)
    return jax.shard_map(
        per_device, mesh=mesh, in_specs=in_specs, out_specs=out_specs, check_vma=False
    )
```

```python
import functools

import jax
import jax.numpy as jnp
from jax import lax
from jax.experimental import pallas as pl
from jax.experimental.pallas import tpu as pltpu
from jax.sharding import PartitionSpec as P

NT = (((1,), (1,)), ((), ()))
CHIPS = [[c + 2 * chip for chip in range(8)] for c in range(2)]
ALONG = (0, 1, 3, 2)
AHEAD = 2
HBM = pl.BlockSpec(memory_space=pltpu.HBM)
VMEM = pl.BlockSpec(memory_space=pltpu.VMEM)


def in_hbm(value):
    return pltpu.with_memory_space_constraint(value, pltpu.HBM)


def limit(mib):
    return pltpu.CompilerParams(vmem_limit_bytes=mib << 20)


def shape(*dims):
    return jax.ShapeDtypeStruct(dims, jnp.float32)


def project_kernel(mine, ahead, acts, grads, *rest):
    if mine:
        held_pin, held_pout, ahead_a, ahead_g, out, held_a, held_g, sem = rest
    else:
        pin, pout, queries, out, passed, held_pin, held_pout, ahead_a, ahead_g, held_a, held_g, sem, p_sem = rest
    examples, rank, rows = out.shape[0], out.shape[1] // 2, out.shape[2]
    t = lax.axis_index("tensor")
    core = t % 2
    part = core if mine else 1 - core

    def spot(u, part):
        return 2 * ((t // 4 + ALONG[u // 2]) % 4) + (t // 2 + part) % 2, pl.ds(u % 2 * rows, rows)

    def fetch(u, part, to_a, to_g, slot):
        e, here = spot(u, part)
        to = pl.ds(slot * rows, rows)
        return [
            pltpu.make_async_copy(grads.at[e, here, :], to_g.at[to, :], sem.at[0, u]),
            pltpu.make_async_copy(acts.at[e, here, :], to_a.at[to, :], sem.at[1, u]),
        ]

    skip = ahead if mine else 0
    blocks = [fetch(e, part, held_a, held_g, e - skip) for e in range(skip, examples)]
    if mine:
        for block in blocks:
            for copy in block:
                copy.start()
    else:
        weights = [
            pltpu.make_async_copy(pout, held_pout, p_sem.at[0]),
            pltpu.make_async_copy(pin, held_pin, p_sem.at[1]),
        ]
        for copy in weights + blocks[0] + blocks[1]:
            copy.start()
        for copy in weights:
            copy.wait()
        for block in blocks[2:6]:
            for copy in block:
                copy.start()

    def push(e, accs, from_a, from_g, slot):
        step = 0
        for rows_in, weights, which in ((from_g, held_pout, 0), (from_a, held_pin, 1)):
            for k in range(weights.shape[1] // 256):
                cut = slice(256 * k, 256 * k + 256)
                for unit in range(2):
                    block = rows_in[pl.ds((slot + unit) * rows, rows), cut]
                    pltpu.matmul_push_rhs(block, step % 2, unit, transpose=True)
                    pltpu.matmul_acc_lhs(accs[2 * unit + which], weights[:, cut], load_staged_rhs=step % 2)
                step += 1

    def pop(e, accs):
        for unit in range(2):
            out[e + unit, :rank, :] = pltpu.matmul_pop(accs[2 * unit])
            out[e + unit, rank:, :] = pltpu.matmul_pop(accs[2 * unit + 1])

    def body(*accs):
        later = []
        for e in range(0, examples, 2):
            turn = accs[4 * (e // 2 % 2) :][:4]
            if e < skip:
                push(e, turn, ahead_a, ahead_g, e)
            else:
                for copy in blocks[e - skip] + blocks[e + 1 - skip]:
                    copy.wait()
                if not mine:
                    for block in blocks[e + 6 : e + 6 + 2]:
                        for copy in block:
                            copy.start()
                if not mine and e + 6 + 2 >= examples and not later:
                    later = [pltpu.make_async_copy(queries, passed, p_sem.at[2])]
                    for k in range(ahead):
                        to = pl.ds(k * rows, rows)
                        at, here = spot(k, core)
                        later.append(pltpu.make_async_copy(grads.at[at, here, :], ahead_g.at[to, :], sem.at[2, k]))
                        later.append(pltpu.make_async_copy(acts.at[at, here, :], ahead_a.at[to, :], sem.at[3, k]))
                    for copy in later:
                        copy.start()
                push(e, turn, held_a, held_g, e - skip)
            if e >= 2:
                pop(e - 2, accs[4 * ((e - 2) // 2 % 2) :][:4])
        pop(examples - 2, accs[4 * ((examples - 2) // 2 % 2) :][:4])
        for copy in later:
            copy.wait()

    units = [pltpu.ACC(unit)((rank, rows), jnp.float32) for _ in range(2) for unit in (0, 0, 1, 1)]
    pl.run_scoped(body, *units)


def project(mine, ahead, acts, grads, *more):
    examples, length, width_in = acts.shape
    width_out = grads.shape[2]
    rows = length // 2
    kept = (examples - ahead if mine else examples) * rows
    out_shape = [pltpu.VMEM((examples, 2 * more[0].shape[0], rows), jnp.float32)]
    scratch_shapes = [
        pltpu.VMEM((kept, width_in), acts.dtype),
        pltpu.VMEM((kept, width_out), grads.dtype),
        pltpu.SemaphoreType.DMA((4, examples)),
    ]
    if not mine:
        pin, pout, queries = more
        out_shape += [pltpu.VMEM(v.shape, v.dtype) for v in (queries, pin, pout)]
        out_shape += [pltpu.VMEM((ahead * rows, v.shape[2]), v.dtype) for v in (acts, grads)]
        scratch_shapes.append(pltpu.SemaphoreType.DMA((3,)))
        more = [in_hbm(v) for v in more]
    return pl.pallas_call(
        functools.partial(project_kernel, mine, ahead),
        out_shape=out_shape,
        in_specs=[HBM] * 2 + [VMEM if mine else HBM] * len(more),
        out_specs=[VMEM] * len(out_shape),
        scratch_shapes=scratch_shapes,
        compiler_params=limit(24),
        name="project_own" if mine else "project_other",
    )(in_hbm(acts), in_hbm(grads), *more)


def merge_kernel(own, got, queries, beside, *outs):
    for k in range(4):
        outs[k][...] = own[2 * k : 2 * k + 2] + got[2 * k : 2 * k + 2]
    pair = outs[4]
    n = queries.shape[0]
    x_hi = lax.axis_index("dp") % 2
    pair[pl.ds(pl.multiple_of(x_hi * n, n), n), :] = queries[...]
    pair[pl.ds(pl.multiple_of((1 - x_hi) * n, n), n), :] = beside[...]


def merge(own, got, queries, beside):
    n, k = queries.shape
    return pl.pallas_call(
        merge_kernel,
        out_shape=[shape(2, *own.shape[1:])] * 4 + [shape(2 * n, k)],
        in_specs=[VMEM] * 4,
        out_specs=[VMEM] * 5,
        compiler_params=limit(8),
        name="merge",
    )(own, got, queries, beside)


def relay_kernel(arrived, pair, out):
    out[...] = pair[...]


def relay(arrived, pair):
    return pl.pallas_call(
        relay_kernel,
        out_shape=shape(*pair.shape),
        in_specs=[pl.BlockSpec(memory_space=pl.ANY), VMEM],
        out_specs=VMEM,
        compiler_params=limit(8),
        name="relay",
    )(arrived, pair)


def halve_kernel(a, b, c, d, keep, send):
    core = lax.axis_index("tensor") % 2
    keep[...] = (a[core] + d[core]) + (b[core] + c[core])
    send[...] = (a[1 - core] + d[1 - core]) + (b[1 - core] + c[1 - core])


def halve(*sides):
    return pl.pallas_call(
        halve_kernel,
        out_shape=[shape(*sides[0].shape[1:])] * 2,
        in_specs=[VMEM] * 4,
        out_specs=[VMEM] * 2,
        compiler_params=limit(8),
        name="halve",
    )(*sides)


def encode_kernel(keep, got, q0, q1, q2, q3, out, near):
    for dy, block in enumerate((q0, q1, q2, q3)):
        near[pl.ds(dy * block.shape[0], block.shape[0]), :] = block[...]
    total = keep[...] + got[...]
    rank = total.shape[0] // 2
    enc = lax.dot_general(
        total[:rank], total[rank:], NT, precision=lax.Precision.HIGHEST, preferred_element_type=jnp.float32
    )
    for t in range(16):
        g = 8 * (t // 2)
        out[t] = jnp.concatenate([enc[g : g + 4, :], enc[g + 4 : g + 8, :]], axis=1)


def encode(keep, got, blocks):
    n, k = blocks[0].shape
    return pl.pallas_call(
        encode_kernel,
        out_shape=[shape(16, 4, 128), shape(4 * n, k)],
        in_specs=[VMEM] * 6,
        out_specs=[VMEM] * 2,
        compiler_params=limit(8),
        name="encode",
    )(keep, got, *blocks)


def score_kernel(scale, slices, near, far, out, tiles):
    core = lax.axis_index("tensor") % 2
    y = lax.axis_index("dp") // 2
    for e in range(8):
        tiles[pl.ds(4 * e, 4), :] = slices[2 * e] + slices[2 * e + 1]
    rows = [tiles[pl.ds(i, 8, stride=4), :] for i in range(4)]
    low = jnp.concatenate([row[:, :64] for row in rows], axis=1)
    high = jnp.concatenate([row[:, 64:] for row in rows], axis=1)
    mine = jnp.where(core == 0, low, high) * scale
    theirs = jnp.where(core == 0, high, low) * scale

    def halves(value):
        high = value.astype(jnp.bfloat16)
        return high, (value - high.astype(jnp.float32)).astype(jnp.bfloat16)

    def dot(enc, block):
        (a, b), (c, d) = halves(enc), halves(block[...])
        both = jnp.concatenate([a, b], axis=0)
        by_high = lax.dot_general(both, c, NT, preferred_element_type=jnp.float32)
        by_low = lax.dot_general(both, d, NT, preferred_element_type=jnp.float32)
        return by_high[:8] + (by_high[8:] + by_low[:8] + by_low[8:])

    part = dot(mine, near) + dot(theirs, far)
    for dy in range(4):
        columns = pl.ds(pl.multiple_of((y - dy + 4) % 4 * 128, 128), 128)
        for g in range(8):
            out[g, :, columns] = part[:, 128 * dy : 128 * dy + 128]


def score(scale, slices, near, far):
    return pl.pallas_call(
        functools.partial(score_kernel, scale),
        out_shape=shape(8, 8, 512),
        in_specs=[VMEM] * 3,
        out_specs=VMEM,
        scratch_shapes=[pltpu.VMEM((32, 128), jnp.float32)],
        compiler_params=limit(8),
        name="score",
    )(slices, near, far)


def to_core(value):
    return lax.ppermute(value, "tensor", [(t, t ^ 1) for t in range(16)])


def to_line(value, dz):
    def to(t):
        return (t + 4 * dz) % 16 ^ (2 * (t % 2))

    return lax.ppermute(value, "tensor", [(t, to(t)) for t in range(16)])


def per_device(acts, grads, proj_in, proj_out, queries):
    length = acts.shape[1]
    rank = proj_in.shape[1]
    pin, pout = proj_in.T, proj_out.T

    with jax.named_scope("sides"):
        other, queries, *first = project(False, AHEAD, acts, grads, pin, pout, queries)
        beside = lax.ppermute(queries, "dp", [(d, d ^ 1) for d in range(8)])
        got = to_core(other)
        (own,) = project(True, AHEAD, acts, grads, *first)
        *sides, pair = merge(own, got, queries, beside)
        sides = [to_line(v, dz) for v, dz in zip(sides, ALONG)]
        pair = relay(sides[0], pair)
        keep, send = halve(*sides)
        got = to_core(send)

    with jax.named_scope("queries"):
        blocks = [pair] + [
            lax.ppermute(pair, "dp", [(d, (d + 2 * dy) % 8) for d in range(8)]) for dy in (1, 2, 3)
        ]

    with jax.named_scope("encode"):
        encoded, near = encode(keep, got, blocks)
        slices = lax.all_to_all(encoded, "tensor", 0, 0, tiled=True)
        far = to_core(near)

    with jax.named_scope("scores"):
        part = score(length ** (-0.5) / rank, slices, near, far)
        parts = lax.all_to_all(part, "tensor", 0, 0, tiled=True, axis_index_groups=CHIPS)
        return jnp.sum(parts, axis=0)


def solution(mesh):
    in_specs = (
        P("dp", None, "tensor"),
        P("dp", None, "tensor"),
        P("tensor", None),
        P("tensor", None),
        P("dp", "tensor"),
    )
    out_specs = P("dp", None)
    return jax.shard_map(
        per_device, mesh=mesh, in_specs=in_specs, out_specs=out_specs, check_vma=False
    )
```
